256 devices in a mesh: pipe: 32 (over y, z_hi, core), dp: 8 (over x, z_lo).
Axes of the slice: x: 4, y: 4, z: 8 (z_hi: 4, z_lo: 2; z = z_hi * 2 + z_lo), core: 2. Of those that a mesh axis runs over, the one named last changes fastest.
Arguments:
- layer_input: bfloat16 [32, 2048, 2048], P('pipe', 'dp'), may hold values from -6 to 6
- out_grad: bfloat16 [32, 2048, 2048], P('pipe', 'dp'), may hold values from -6 to 6
- w_in: bfloat16 [32, 2048, 2, 2048], P('pipe', 'dp'), may hold values from -0.125 to 0.125
- w_out: bfloat16 [32, 2048, 2, 1024], P('pipe', 'dp'), may hold values from -0.1875 to 0.1875
- slots: int32 [32, 8, 2, 128], P('pipe', 'dp'), may hold values from 0 to 255, as said below
- counts: int32 [32, 8, 2], P('pipe', 'dp'), may hold values from 32 to 128, as said below
- probs: float32 [32, 8, 2, 128], P('pipe', 'dp'), may hold values from 0.1 to 1
Outputs:
- handed_grad: bfloat16 [32, 2048, 2048], P('pipe', 'dp')
- grad_in: bfloat16 [32, 2048, 2, 2048], P('pipe', 'dp')
- grad_out: bfloat16 [32, 2048, 2, 1024], P('pipe', 'dp')
- router_grad: float32 [32, 8, 2, 128], P('pipe', 'dp')
The draws below stay inside these ranges and needn't reach their ends.
Inputs may be any that keep to these rules, and one draw needn't show every extreme that they name: `slots`: for each section, replica and expert the 128 entries are distinct local token indices; the first counts entries are the tokens routed to that expert, the others are unused. `counts`: some expert on some replica has all 128 slots in use in every draw.
All inputs are finite; a program needn't handle non-finite values.
Results may differ from the reference program's by a relative error of at most 0.017.
Values may be sent and summed in bfloat16 or wider, within the bound.
No kernel may reach another device: no remote copies, remote signals or barrier semaphores. Data moves between devices by JAX's collectives and lax.ppermute only.
A program may use at most 192 MiB of HBM per device.

```python
import jax
import jax.numpy as jnp
from jax import lax

D = 2048
HID = 1024
EXP_WIN = 2
TOK_DEV = 256
CAP = 128
SECTIONS = 32
REPLICAS = 8
TOKENS = 2048


def draw_slots(key, part):
    key = jax.random.fold_in(key, 11)
    shape = (SECTIONS, REPLICAS, EXP_WIN, TOK_DEV)
    scores = jax.random.randint(key, shape, 0, 1 << 20)
    order = scores * TOK_DEV + lax.broadcasted_iota(jnp.int32, shape, 3)
    perm = jnp.argsort(order, axis=-1).astype(jnp.int32)
    return perm[..., :CAP]


def draw_counts(key, part):
    key = jax.random.fold_in(key, 23)
    first, second = jax.random.split(key)
    shape = (SECTIONS, REPLICAS, EXP_WIN)
    values = jax.random.randint(first, shape, CAP // 4, CAP + 1)
    chosen = jax.random.randint(second, (), 0, SECTIONS * REPLICAS * EXP_WIN)
    flat = lax.broadcasted_iota(jnp.int32, (SECTIONS * REPLICAS * EXP_WIN,), 0).reshape(shape)
    return jnp.where(flat == chosen, CAP, values).astype(jnp.int32)


def steps_of(own_key, shape, pieces, smallest, top_value):
    def one(axis_at, blocks):
        heights = jax.random.uniform(jax.random.fold_in(jax.random.fold_in(own_key, 6), axis_at), (blocks,), jnp.float32, smallest / len(pieces), top_value / len(pieces))
        return jnp.repeat(jnp.exp(heights), shape[axis_at] // blocks).reshape((-1,) + (1,) * (len(shape) - axis_at - 1))

    gain = one(*pieces[0])
    for cut in pieces[1:]:
        gain = gain * one(*cut)
    return gain


def noise(own_key, shape, deviation, limit, cuts=(), held_as=jnp.bfloat16):
    array = jax.random.normal(own_key, shape, jnp.float32) * deviation
    if len(cuts) > 0:
        array = steps_of(own_key, shape, cuts, -0.22, 0.18) * array
    return jnp.clip(array, min=-limit, max=limit).astype(held_as)


def setup_inputs(seed: int = 0) -> dict:
    key_of = jax.random.split(jax.random.key(seed), 8)
    return {
        "layer_input": noise(key_of[0], (SECTIONS, TOKENS, D), 1.0, 6.0, ((0, 32), (1, 8))),
        "out_grad": noise(key_of[1], (SECTIONS, TOKENS, D), 1.0, 6.0, ((0, 32), (1, 8))),
        "w_in": noise(key_of[2], (SECTIONS, D, EXP_WIN, 2 * HID), D ** -0.5, 0.125, ((0, 32), (1, 8))),
        "w_out": noise(key_of[3], (SECTIONS, D, EXP_WIN, HID), HID ** -0.5, 0.1875, ((0, 32), (1, 8))),
        "slots": draw_slots(jax.random.fold_in(key_of[7], 71), 0),
        "counts": draw_counts(jax.random.fold_in(key_of[7], 71), 0),
        "probs": jnp.clip(0.1 + 0.9 * jax.random.uniform(key_of[6], (SECTIONS, REPLICAS, EXP_WIN, CAP), jnp.float32) ** steps_of(key_of[6], (SECTIONS, REPLICAS, EXP_WIN, CAP), ((0, 32), (1, 8)), -0.2, 0.2), 0.1, 1.0),
    }


def one_section(inputs):
    x_section, dy_section, win, wout, slot_rows, slot_counts, slot_probs = inputs
    wide = win.shape[-1] // 2
    offset = lax.broadcasted_iota(jnp.int32, slot_rows.shape, 0) * TOK_DEV
    rows = (slot_rows + offset).astype(jnp.int32)
    live = lax.broadcasted_iota(jnp.int32, slot_rows.shape, 2) < slot_counts[..., None]
    weight = jnp.where(live, slot_probs, jnp.zeros_like(slot_probs))
    picked = x_section[rows].astype(jnp.float32)
    picked_grad = dy_section[rows].astype(jnp.float32)
    pre = jnp.einsum("recd,dek->reck", picked, win.astype(jnp.float32))
    gate = pre[..., :wide]
    upper = pre[..., wide:]
    sig = jax.nn.sigmoid(gate)
    act = (gate * sig * upper).astype(jnp.bfloat16).astype(jnp.float32)
    expert_output = jnp.einsum("reck,dek->recd", act, wout.astype(jnp.float32))
    router = jnp.where(live, jnp.sum(picked_grad * expert_output, axis=-1), jnp.zeros_like(slot_probs))
    scaled = (weight[..., None] * picked_grad).astype(jnp.bfloat16).astype(jnp.float32)
    back = jnp.einsum("recd,dek->reck", scaled, wout.astype(jnp.float32))
    dgate = back * upper * sig * (1.0 + gate * (1.0 - sig))
    dupper = back * gate * sig
    dpre = jnp.concatenate([dgate, dupper], axis=-1).astype(jnp.bfloat16).astype(jnp.float32)
    slot_grad = jnp.einsum("reck,dek->recd", dpre, win.astype(jnp.float32))
    contrib = jnp.zeros(dy_section.shape, jnp.float32).at[rows.reshape(-1)].add(slot_grad.reshape(-1, slot_grad.shape[-1]))
    through = (dy_section.astype(jnp.float32) + contrib).astype(jnp.bfloat16)
    part_in = jnp.einsum("recd,reck->rdek", picked, dpre)
    part_in = lax.optimization_barrier(part_in.astype(jnp.bfloat16)).astype(jnp.float32)
    part_out = jnp.einsum("recd,reck->rdek", scaled, act)
    part_out = lax.optimization_barrier(part_out.astype(jnp.bfloat16)).astype(jnp.float32)
    grad_in = jnp.sum(part_in, axis=0).astype(jnp.bfloat16)
    grad_out = jnp.sum(part_out, axis=0).astype(jnp.bfloat16)
    return through, grad_in, grad_out, router


def reference(layer_input, out_grad, w_in, w_out, slots, counts, probs):
    through, grad_in, grad_out, router = lax.map(one_section, (layer_input, out_grad, w_in, w_out, slots, counts, probs))
    handed_grad = jnp.roll(through, -1, axis=0)
    return handed_grad, grad_in, grad_out, router
```

```python
import jax
import jax.numpy as jnp
from jax import lax
from jax.sharding import PartitionSpec as P

F32 = jnp.float32
BF16 = jnp.bfloat16

RANK_OF_CODE = (0, 1, 2, 3, 6, 7, 4, 5)
CODE_OF_RANK = (0, 1, 2, 3, 6, 7, 4, 5)
BIT_A, BIT_B, BIT_Z = 4, 2, 1
ROLES = ((BIT_A, BIT_B), (BIT_B, BIT_A))
CHUNKS = 2


def flipped(value, bits):
    pairs = [(r, RANK_OF_CODE[CODE_OF_RANK[r] ^ bits]) for r in range(8)]
    return lax.ppermute(value, "dp", pairs)


def per_device(layer_input, out_grad, w_in, w_out, slots, counts, probs):
    tokens = layer_input[0]
    grads = out_grad[0]
    routed = slots[0, 0]
    experts, cap = routed.shape
    rows, width = tokens.shape
    hid = w_out.shape[-1]
    part = width // 8
    step = hid // CHUNKS
    live = lax.broadcasted_iota(jnp.int32, routed.shape, 1) < counts[0, 0][:, None]
    weight = jnp.where(live, probs[0, 0], jnp.zeros_like(probs[0, 0]))
    code = jnp.asarray(CODE_OF_RANK, jnp.int32)[lax.axis_index("dp")]
    rank_at = [jnp.asarray(RANK_OF_CODE, jnp.int32)[code ^ bits] for bits in range(8)]

    def columns(array, bits):
        return lax.dynamic_slice(array, (0, rank_at[bits] * part), (array.shape[0], part))

    sides = []
    for e in range(experts):
        pair, swap = ROLES[e]
        members = (0, BIT_Z, swap, swap | BIT_Z)
        both = jnp.concatenate(
            [jnp.take(tokens, routed[e], axis=0), jnp.take(grads, routed[e], axis=0)], axis=0
        )
        got = []
        for m in members:
            piece = jnp.concatenate([columns(both, m), columns(both, m | pair)], axis=1)
            got.append(piece if m == 0 else flipped(piece, m))
        x_all = jnp.concatenate([g[:cap] for g in got], axis=0)
        y_all = jnp.concatenate([g[cap:] for g in got], axis=0)
        sides.append((pair, swap, members, x_all, y_all))

    weights = {}
    for c in range(CHUNKS):
        for e in range(experts):
            low = c * step
            own = jnp.concatenate(
                [
                    w_in[0, :, e, low : low + step],
                    w_in[0, :, e, hid + low : hid + low + step],
                    w_out[0, :, e, low : low + step],
                ],
                axis=1,
            )
            weights[c, e] = jnp.concatenate([own, flipped(own, sides[e][0])], axis=0)

    slot_grad = [0.0] * experts
    router = [0.0] * experts
    out_parts = {}
    for c in range(CHUNKS):
        for e in range(experts):
            pair, swap, members, x_all, y_all = sides[e]
            full = weights[c, e]
            partial = jnp.concatenate(
                [
                    jnp.dot(x_all, full[:, : 2 * step], preferred_element_type=F32),
                    jnp.dot(y_all, full[:, 2 * step :], preferred_element_type=F32),
                ],
                axis=1,
            )
            half = 2 * cap
            got = flipped(partial[half:].astype(BF16), swap)
            partial = partial[:half] + got.astype(F32)
            got = flipped(partial[cap:].astype(BF16), BIT_Z)
            sums = partial[:cap] + got.astype(F32)
            gate, upper, raw = sums[:, :step], sums[:, step : 2 * step], sums[:, 2 * step :]
            sig = jax.nn.sigmoid(gate)
            act = gate * sig * upper
            scale = weight[e][:, None]
            back = raw * scale
            router[e] += jnp.sum(act.astype(BF16).astype(F32) * raw, axis=-1)
            mine = jnp.concatenate(
                [back * upper * sig * (1.0 + gate * (1.0 - sig)), back * gate * sig, act * scale],
                axis=1,
            ).astype(BF16)
            mine = jnp.concatenate([mine, flipped(mine, BIT_Z)], axis=0)
            every = jnp.concatenate([mine, flipped(mine, swap)], axis=0)
            dpre, wact = every[:, : 2 * step], every[:, 2 * step :]
            term = jnp.concatenate(
                [
                    jnp.einsum("sd,sk->dk", x_all, dpre, preferred_element_type=F32),
                    jnp.einsum("sd,sk->dk", y_all, wact, preferred_element_type=F32),
                ],
                axis=1,
            )
            slot_grad[e] += jnp.einsum("sk,dk->sd", dpre, full[:, : 2 * step], preferred_element_type=F32)
            got = flipped(term[part:].astype(BF16), pair)
            out_parts[c, e] = (term[:part] + got.astype(F32)).astype(BF16)

    through = grads.astype(F32)
    for e in range(experts):
        pair, swap, members, _, _ = sides[e]
        low = slot_grad[e].astype(BF16)
        whole = jnp.zeros((cap, width), BF16)
        for i, m in enumerate(members):
            piece = low[i * cap : (i + 1) * cap]
            if m:
                piece = flipped(piece, m)
            whole = lax.dynamic_update_slice(whole, piece[:, :part], (0, rank_at[m] * part))
            whole = lax.dynamic_update_slice(whole, piece[:, part:], (0, rank_at[m | pair] * part))
        hot = (lax.broadcasted_iota(jnp.int32, (rows, cap), 0) == routed[e][None, :]).astype(BF16)
        through += jnp.dot(hot, whole, preferred_element_type=F32)
    through = through.astype(BF16)
    sections = lax.axis_size("pipe")
    handed = lax.ppermute(through, "pipe", [(i, (i - 1) % sections) for i in range(sections)])

    grad_in, grad_out = [], []
    for e in range(experts):
        grad_in.append(
            jnp.concatenate(
                [out_parts[c, e][:, :step] for c in range(CHUNKS)]
                + [out_parts[c, e][:, step : 2 * step] for c in range(CHUNKS)],
                axis=1,
            )
        )
        grad_out.append(jnp.concatenate([out_parts[c, e][:, 2 * step :] for c in range(CHUNKS)], axis=1))
    router_grad = jnp.where(live, jnp.stack(router), jnp.zeros_like(weight))
    return (
        handed[None],
        jnp.stack(grad_in, axis=1)[None],
        jnp.stack(grad_out, axis=1)[None],
        router_grad[None, None],
    )


def solution(mesh):
    return jax.shard_map(
        per_device,
        mesh=mesh,
        in_specs=(
            P("pipe", "dp", None),
            P("pipe", "dp", None),
            P("pipe", "dp", None, None),
            P("pipe", "dp", None, None),
            P("pipe", "dp", None, None),
            P("pipe", "dp", None),
            P("pipe", "dp", None, None),
        ),
        out_specs=(
            P("pipe", "dp", None),
            P("pipe", "dp", None, None),
            P("pipe", "dp", None, None),
            P("pipe", "dp", None, None),
        ),
        check_vma=False,
    )
```

```python
import jax
import jax.numpy as jnp
from jax import lax
from jax.experimental import pallas as pl
from jax.experimental.pallas import tpu as pltpu
from jax.sharding import PartitionSpec as P

F32 = jnp.float32
BF16 = jnp.bfloat16

BIT_A, BIT_B, BIT_Z = 4, 2, 1
ROLES = ((BIT_A, BIT_B), (BIT_B, BIT_A))
CHUNKS = 4
FIRST = 2
JOINS = ((0, 1, 2), (3,))


def gray(index):
    return index ^ ((index & 4) >> 1)


def flipped(value, bits):
    return lax.ppermute(value, "dp", [(r, gray(gray(r) ^ bits)) for r in range(8)])


class Order:
    def __init__(self):
        self.taken = []
        self.last = None

    def take(self, *results):
        self.taken += results

    def held(self, value):
        return lax.optimization_barrier((value, self.last))[0]

    def send(self, value, bits, axis="dp"):
        others = self.taken + ([] if self.last is None else [self.last])
        value, *_ = lax.optimization_barrier((value, *others))
        self.last, self.taken = value, []
        if axis == "dp":
            return flipped(value, bits)
        peers = lax.axis_size(axis)
        return lax.ppermute(value, axis, [(i, (i + bits) % peers) for i in range(peers)])


def dot(a, b, dims=((1,), (0,))):
    return lax.dot_general(a, b, (dims, ((), ())), preferred_element_type=F32)


def pick_kernel(slots_ref, x_ref, y_ref, win_ref, wout_ref, *outs):
    z_ref, far_refs, mix_refs, near_refs = outs[0], outs[1:3], outs[3:5], outs[5:7]
    rows, width = x_ref.shape
    experts, cap = slots_ref.shape
    part = width // 8
    hid = wout_ref.shape[-1]
    step = hid // CHUNKS
    code = gray(lax.axis_index("dp"))

    def put(ref, row, e, member):
        token = lax.broadcasted_iota(jnp.int32, (rows, cap), 0)
        hot = (token == slots_ref[e][None, :]).astype(F32).T.astype(BF16)
        for m in (member, member | ROLES[e][0]):
            low = pl.multiple_of(gray(code ^ m) * part, part)
            for source in (x_ref, y_ref):
                ref[row : row + cap] = dot(hot, source[:, pl.ds(low, part)]).astype(BF16)
                row += cap

    for e, (pair, swap) in enumerate(ROLES):
        put(z_ref, 4 * cap * e, e, BIT_Z)
        put(far_refs[e], 0, e, swap | BIT_Z)
        put(near_refs[e], 0, e, 0)
        put(mix_refs[e], 0, 1 - e, pair)
        for c in range(FIRST):
            put_weights(mix_refs[e], 4 * cap + 3 * rows * c, win_ref, wout_ref, e, c * step, step)


def put_weights(ref, row, win_ref, wout_ref, e, low, step):
    rows = win_ref.shape[0]
    at = lax.broadcasted_iota(jnp.int32, (rows, 2 * rows), 0)
    of = lax.broadcasted_iota(jnp.int32, (rows, 2 * rows), 1)
    chosen = (of == 2 * at + e).astype(BF16)
    hid = wout_ref.shape[-1]
    for source, col in ((win_ref, low), (win_ref, hid + low), (wout_ref, low)):
        both = source[:, :, col : col + step].reshape(2 * rows, step)
        ref[row : row + rows] = dot(chosen, both).astype(BF16)
        row += rows


def split_kernel(win_ref, wout_ref, *outs):
    step = wout_ref.shape[-1] // CHUNKS
    for c in range(FIRST, CHUNKS):
        for e in range(2):
            put_weights(outs[2 * (c - FIRST) + e], 0, win_ref, wout_ref, e, c * step, step)


def kernel_call(kernel, shapes, *operands):
    return pl.pallas_call(
        kernel,
        out_shape=[jax.ShapeDtypeStruct(shape, BF16) for shape in shapes],
        compiler_params=pltpu.CompilerParams(vmem_limit_bytes=40 * 2**20),
        cost_estimate=pl.CostEstimate(flops=10**9, bytes_accessed=6 * 2**20, transcendentals=0),
    )(*operands)


def join_chunks(which, terms, hid, earlier):
    step = hid // CHUNKS
    rows = terms[which[0], 0][0].shape[0]
    parts = [terms[c, e][i] for c in which for i in range(3) for e in range(2)]
    copies = 3 * len(which)

    def kernel(*refs):
        ins = refs[: len(parts)]
        to_in, to_out, held, done = refs[len(parts) + len(earlier) :]
        at = lax.broadcasted_iota(jnp.int32, (2 * rows, rows), 0)
        of = lax.broadcasted_iota(jnp.int32, (2 * rows, rows), 1)
        even, odd = (at == 2 * of).astype(BF16), (at == 2 * of + 1).astype(BF16)
        started = []
        for n in range(copies):
            c, i = which[n // 3], n % 3
            both = dot(even, ins[2 * n][...]) + dot(odd, ins[2 * n + 1][...])
            held[n] = both.astype(BF16).reshape(rows, 2, step)
            target = to_in.at[:, :, pl.ds(i * hid + c * step, step)] if i < 2 else to_out.at[:, :, pl.ds(c * step, step)]
            copy = pltpu.make_async_copy(held.at[n], target, done.at[n])
            copy.start()
            started.append(copy)
        for copy in started:
            copy.wait()

    anywhere = pl.BlockSpec(memory_space=pl.ANY)
    inside = pl.BlockSpec(memory_space=pltpu.VMEM)
    return pl.pallas_call(
        kernel,
        out_shape=[jax.ShapeDtypeStruct((rows, 2, n), BF16) for n in (2 * hid, hid)],
        in_specs=[inside] * len(parts) + [anywhere] * len(earlier),
        out_specs=[anywhere] * 2,
        scratch_shapes=[pltpu.VMEM((copies, rows, 2, step), BF16), pltpu.SemaphoreType.DMA((copies,))],
        input_output_aliases={len(parts) + i: i for i in range(len(earlier))},
        compiler_params=pltpu.CompilerParams(vmem_limit_bytes=40 * 2**20),
        cost_estimate=pl.CostEstimate(flops=10**9, bytes_accessed=4 * 2**20, transcendentals=0),
    )(*parts, *earlier)


def per_device(layer_input, out_grad, w_in, w_out, slots, counts, probs):
    tokens = layer_input[0]
    grads = out_grad[0]
    routed = slots[0, 0]
    experts, cap = routed.shape
    rows, width = tokens.shape
    hid = w_out.shape[-1]
    part = width // 8
    step = hid // CHUNKS
    pairs = [r[0] for r in ROLES]
    swaps = [r[1] for r in ROLES]
    members = [(0, BIT_Z, s, s | BIT_Z) for s in swaps]
    each = range(experts)
    chunks = range(CHUNKS)
    order = Order()
    live = lax.broadcasted_iota(jnp.int32, routed.shape, 1) < counts[0, 0][:, None]
    weight = jnp.where(live, probs[0, 0], jnp.zeros_like(probs[0, 0]))
    code = gray(lax.axis_index("dp"))
    place = [gray(code ^ bits) * part for bits in range(8)]

    hot = [
        (lax.broadcasted_iota(jnp.int32, (rows, cap), 0) == routed[e][None, :]).astype(BF16)
        for e in each
    ]
    size = 4 * cap
    z_piece, far_a, far_b, mixed_a, mixed_b, near_a, near_b = kernel_call(
        pick_kernel,
        [(2 * size, part)] + [(size, part)] * 2 + [(size + 3 * part * FIRST, part)] * 2 + [(size, part)] * 2,
        routed, tokens, grads, w_in[0], w_out[0],
    )
    split = kernel_call(split_kernel, [(3 * part, part)] * (2 * (CHUNKS - FIRST)), w_in[0], w_out[0])

    def first_weights(mixed, c):
        return mixed[size + 3 * part * c : size + 3 * part * (c + 1)]

    own = {}
    for c in chunks:
        for e, mixed in enumerate((mixed_a, mixed_b)):
            own[c, e] = first_weights(mixed, c) if c < FIRST else split[2 * (c - FIRST) + e]
    got, moved = {(0, 0): near_a, (1, 0): near_b}, {}
    for e, piece in enumerate((mixed_a, mixed_b)):
        mixed = order.send(piece, pairs[e])
        got[1 - e, pairs[e]] = mixed[:size]
        for c in range(FIRST):
            moved[c, e] = first_weights(mixed, c)
    bundle = order.send(z_piece, BIT_Z)
    for e, piece in enumerate((far_a, far_b)):
        got[e, BIT_Z] = bundle[size * e : size * (e + 1)]
        got[e, swaps[e] | BIT_Z] = order.send(piece, swaps[e] | BIT_Z)
    order.take(bundle, *got.values())

    def gathered(e, low):
        return jnp.concatenate(
            [
                jnp.concatenate([got[e, m][low : low + cap], got[e, m][low + 2 * cap : low + 3 * cap]], axis=1)
                for m in members[e]
            ],
            axis=0,
        )

    x_all, y_all = [None] * experts, [None] * experts

    full, near, far_sums, z_sums, mine, theirs = {}, {}, {}, {}, {}, {}
    two, four, every, terms, sent_terms, arrived = {}, {}, {}, {}, {}, {}
    router = [0.0] * experts
    slot_sum = [0.0] * experts

    def send_weights(*which):
        rows_of = 3 * part
        for e in each:
            block = order.send(jnp.concatenate([own[c, e] for c in which], axis=0), pairs[e])
            for i, c in enumerate(which):
                moved[c, e] = block[i * rows_of : (i + 1) * rows_of]

    def take(table, *which):
        order.take(*[table[c, e] for c in which for e in each])

    def partials(c):
        for e in each:
            if c == 0:
                got[e, 0] = order.held(got[e, 0])
                x_all[e], y_all[e] = gathered(e, 0), gathered(e, cap)
            other = order.held(moved[c, e])
            blocks = [
                jnp.concatenate([t[i * part : (i + 1) * part] for t in (own[c, e], other)], axis=0)
                for i in range(3)
            ]
            full[c, e] = blocks
            partial = [dot(x_all[e], blocks[0]), dot(x_all[e], blocks[1]), dot(y_all[e], blocks[2])]
            near[c, e] = [p[: 2 * cap] for p in partial]
            far = jnp.concatenate([p[2 * cap :].astype(BF16) for p in partial], axis=0)
            far_sums[c, e] = order.send(far, swaps[e])

    def second_sums(c):
        take(far_sums, c)
        for e in each:
            near[c, e] = [
                p + far_sums[c, e][2 * cap * i : 2 * cap * (i + 1)].astype(F32)
                for i, p in enumerate(near[c, e])
            ]
        far = jnp.concatenate([p[cap:].astype(BF16) for e in each for p in near[c, e]], axis=0)
        z_sums[c] = order.send(far, BIT_Z)

    def activate(c):
        order.take(z_sums[c])
        parts = []
        for e in each:
            gate, upper, raw = [
                p[:cap] + z_sums[c][(3 * e + i) * cap : (3 * e + i + 1) * cap].astype(F32)
                for i, p in enumerate(near[c, e])
            ]
            sig = jax.nn.sigmoid(gate)
            act = gate * sig * upper
            scale = weight[e][:, None]
            back = raw * scale
            router[e] += jnp.sum(act.astype(BF16).astype(F32) * raw, axis=-1)
            parts += [back * upper * sig * (1.0 + gate * (1.0 - sig)), back * gate * sig, act * scale]
        mine[c] = jnp.concatenate([m.astype(BF16) for m in parts], axis=0)
        theirs[c] = order.send(mine[c], BIT_Z)

    def spread(*which):
        order.take(*[theirs[c] for c in which])
        rows_of = 6 * cap
        for e in each:
            for c in which:
                two[c, e] = jnp.concatenate(
                    [t[3 * cap * e : 3 * cap * (e + 1)].reshape(3, cap, step) for t in (mine[c], theirs[c])],
                    axis=1,
                )
            flat = jnp.concatenate([two[c, e].reshape(-1, step) for c in which], axis=0)
            block = order.send(flat, swaps[e])
            arrived[which, e] = block
            for i, c in enumerate(which):
                four[c, e] = block[i * rows_of : (i + 1) * rows_of]

    down = ((0,), (0,))

    def collect(*which):
        order.take(*[arrived[which, e] for e in each])
        for c in which:
            for e in each:
                every[c, e] = jnp.concatenate([two[c, e], four[c, e].reshape(3, 2 * cap, step)], axis=1)
                for i in range(2):
                    slot_sum[e] += dot(every[c, e][i], full[c, e][i], ((1,), (1,)))

    def weight_grads(*which):
        for e in each:
            far = []
            for c in which:
                dgate, dupper, wact = every[c, e]
                terms[c, e] = [dot(x_all[e], dgate, down), dot(x_all[e], dupper, down), dot(y_all[e], wact, down)]
                far += [t[part:].astype(BF16) for t in terms[c, e]]
            block = order.send(jnp.concatenate(far, axis=0), pairs[e])
            sent_terms[which, e] = block
            for i, c in enumerate(which):
                terms[c, e] = [
                    (t[:part] + block[(3 * i + j) * part : (3 * i + j + 1) * part].astype(F32)).astype(BF16)
                    for j, t in enumerate(terms[c, e])
                ]

    back = {}

    def send_back():
        low = [slot_sum[e].astype(BF16) for e in each]
        bundle = order.send(jnp.concatenate([low[e][cap : 2 * cap] for e in each], axis=0), BIT_Z)
        order_taken = [bundle]
        for i in (3, 2):
            for e in each:
                m = members[e][i]
                back[e, m] = order.send(low[e][i * cap : (i + 1) * cap], m)
                order_taken.append(back[e, m])
        for e in each:
            back[e, 0] = low[e][:cap]
            back[e, BIT_Z] = bundle[cap * e : cap * (e + 1)]
        order.take(*order_taken)

    def hand_over():
        through = grads.astype(F32)
        for e in each:
            whole = jnp.zeros((cap, width), BF16)
            for m in members[e]:
                whole = lax.dynamic_update_slice(whole, back[e, m][:, :part], (0, place[m]))
                whole = lax.dynamic_update_slice(whole, back[e, m][:, part:], (0, place[m | pairs[e]]))
            through += dot(hot[e], whole)
        return order.send(through.astype(BF16), -1, "pipe")


    partials(0)
    send_weights(2)
    second_sums(0)
    partials(1)
    activate(0)
    take(moved, 2)
    send_weights(3)
    second_sums(1)
    order.take(theirs[0])
    partials(2)
    activate(1)
    take(moved, 3)
    second_sums(2)
    partials(3)
    spread(0, 1)
    activate(2)
    second_sums(3)
    spread(2)
    activate(3)
    collect(0, 1)
    weight_grads(0)
    spread(3)
    collect(2)
    collect(3)
    order.take(sent_terms[(0,), 0], sent_terms[(0,), 1])
    send_back()
    handed = hand_over()
    weight_grads(1, 2)
    weight_grads(3)

    joined = ()
    for which in JOINS:
        joined = join_chunks(which, terms, hid, joined)
    router_grad = jnp.where(live, jnp.stack(router), jnp.zeros_like(weight))
    return (
        handed[None],
        joined[0][None],
        joined[1][None],
        router_grad[None, None],
    )


def solution(mesh):
    return jax.shard_map(
        per_device,
        mesh=mesh,
        in_specs=(
            P("pipe", "dp", None),
            P("pipe", "dp", None),
            P("pipe", "dp", None, None),
            P("pipe", "dp", None, None),
            P("pipe", "dp", None, None),
            P("pipe", "dp", None),
            P("pipe", "dp", None, None),
        ),
        out_specs=(
            P("pipe", "dp", None),
            P("pipe", "dp", None, None),
            P("pipe", "dp", None, None),
            P("pipe", "dp", None, None),
        ),
        check_vma=False,
    )
```

```python
import jax
import jax.numpy as jnp
from jax import lax
from jax.experimental import pallas as pl
from jax.experimental.pallas import tpu as pltpu
from jax.sharding import PartitionSpec as P

F32 = jnp.float32
BF16 = jnp.bfloat16

BIT_A, BIT_B, BIT_Z = 4, 2, 1
ROLES = ((BIT_A, BIT_B), (BIT_B, BIT_A))
CHUNKS = 4
FIRST = 2
JOINS = ((0, 1, 2), (3,))


def gray(index):
    return index ^ ((index & 4) >> 1)


def flipped(value, bits):
    return lax.ppermute(value, "dp", [(r, gray(gray(r) ^ bits)) for r in range(8)])


class Order:
    def __init__(self):
        self.taken = []
        self.last = None

    def take(self, *results):
        self.taken += results

    def held(self, value):
        return lax.optimization_barrier((value, self.last))[0]

    def send(self, value, bits, axis="dp"):
        others = self.taken + ([] if self.last is None else [self.last])
        value, *_ = lax.optimization_barrier((value, *others))
        self.last, self.taken = value, []
        if axis == "dp":
            return flipped(value, bits)
        peers = lax.axis_size(axis)
        return lax.ppermute(value, axis, [(i, (i + bits) % peers) for i in range(peers)])


def dot(a, b, dims=((1,), (0,))):
    return lax.dot_general(a, b, (dims, ((), ())), preferred_element_type=F32)


def pick_kernel(slots_ref, x_ref, y_ref, win_ref, wout_ref, *outs):
    z_ref, far_refs, mix_refs, near_refs = outs[0], outs[1:3], outs[3:5], outs[5:7]
    rows, width = x_ref.shape
    experts, cap = slots_ref.shape
    part = width // 8
    hid = wout_ref.shape[-1]
    step = hid // CHUNKS
    code = gray(lax.axis_index("dp"))

    def put(ref, row, e, member):
        token = lax.broadcasted_iota(jnp.int32, (rows, cap), 0)
        hot = (token == slots_ref[e][None, :]).astype(F32).T.astype(BF16)
        for m in (member, member | ROLES[e][0]):
            low = pl.multiple_of(gray(code ^ m) * part, part)
            for source in (x_ref, y_ref):
                ref[row : row + cap] = dot(hot, source[:, pl.ds(low, part)]).astype(BF16)
                row += cap

    for e, (pair, swap) in enumerate(ROLES):
        put(z_ref, 4 * cap * e, e, BIT_Z)
        put(far_refs[e], 0, e, swap | BIT_Z)
        put(near_refs[e], 0, e, 0)
        put(mix_refs[e], 0, 1 - e, pair)
        for c in range(FIRST):
            put_weights(mix_refs[e], 4 * cap + 3 * rows * c, win_ref, wout_ref, e, c * step, step)


def put_weights(ref, row, win_ref, wout_ref, e, low, step):
    rows = win_ref.shape[0]
    at = lax.broadcasted_iota(jnp.int32, (rows, 2 * rows), 0)
    of = lax.broadcasted_iota(jnp.int32, (rows, 2 * rows), 1)
    chosen = (of == 2 * at + e).astype(BF16)
    hid = wout_ref.shape[-1]
    for source, col in ((win_ref, low), (win_ref, hid + low), (wout_ref, low)):
        both = source[:, :, col : col + step].reshape(2 * rows, step)
        ref[row : row + rows] = dot(chosen, both).astype(BF16)
        row += rows


def split_kernel(win_ref, wout_ref, *outs):
    step = wout_ref.shape[-1] // CHUNKS
    for c in range(FIRST, CHUNKS):
        for e in range(2):
            put_weights(outs[2 * (c - FIRST) + e], 0, win_ref, wout_ref, e, c * step, step)


def kernel_call(kernel, shapes, *operands):
    return pl.pallas_call(
        kernel,
        out_shape=[jax.ShapeDtypeStruct(shape, BF16) for shape in shapes],
        compiler_params=pltpu.CompilerParams(vmem_limit_bytes=40 * 2**20),
        cost_estimate=pl.CostEstimate(flops=10**9, bytes_accessed=6 * 2**20, transcendentals=0),
    )(*operands)


def join_chunks(which, terms, hid, earlier):
    step = hid // CHUNKS
    rows = terms[which[0], 0][0].shape[0]
    parts = [terms[c, e][i] for c in which for i in range(3) for e in range(2)]
    copies = 3 * len(which)

    def kernel(*refs):
        ins = refs[: len(parts)]
        to_in, to_out, held, done = refs[len(parts) + len(earlier) :]
        at = lax.broadcasted_iota(jnp.int32, (2 * rows, rows), 0)
        of = lax.broadcasted_iota(jnp.int32, (2 * rows, rows), 1)
        even, odd = (at == 2 * of).astype(BF16), (at == 2 * of + 1).astype(BF16)
        started = []
        for n in range(copies):
            c, i = which[n // 3], n % 3
            both = dot(even, ins[2 * n][...]) + dot(odd, ins[2 * n + 1][...])
            held[n] = both.astype(BF16).reshape(rows, 2, step)
            target = to_in.at[:, :, pl.ds(i * hid + c * step, step)] if i < 2 else to_out.at[:, :, pl.ds(c * step, step)]
            copy = pltpu.make_async_copy(held.at[n], target, done.at[n])
            copy.start()
            started.append(copy)
        for copy in started:
            copy.wait()

    anywhere = pl.BlockSpec(memory_space=pl.ANY)
    inside = pl.BlockSpec(memory_space=pltpu.VMEM)
    return pl.pallas_call(
        kernel,
        out_shape=[jax.ShapeDtypeStruct((rows, 2, n), BF16) for n in (2 * hid, hid)],
        in_specs=[inside] * len(parts) + [anywhere] * len(earlier),
        out_specs=[anywhere] * 2,
        scratch_shapes=[pltpu.VMEM((copies, rows, 2, step), BF16), pltpu.SemaphoreType.DMA((copies,))],
        input_output_aliases={len(parts) + i: i for i in range(len(earlier))},
        compiler_params=pltpu.CompilerParams(vmem_limit_bytes=40 * 2**20),
        cost_estimate=pl.CostEstimate(flops=10**9, bytes_accessed=4 * 2**20, transcendentals=0),
    )(*parts, *earlier)


def per_device(layer_input, out_grad, w_in, w_out, slots, counts, probs):
    tokens = layer_input[0]
    grads = out_grad[0]
    routed = slots[0, 0]
    experts, cap = routed.shape
    rows, width = tokens.shape
    hid = w_out.shape[-1]
    part = width // 8
    step = hid // CHUNKS
    pairs = [r[0] for r in ROLES]
    swaps = [r[1] for r in ROLES]
    members = [(0, BIT_Z, s, s | BIT_Z) for s in swaps]
    each = range(experts)
    chunks = range(CHUNKS)
    order = Order()
    live = lax.broadcasted_iota(jnp.int32, routed.shape, 1) < counts[0, 0][:, None]
    weight = jnp.where(live, probs[0, 0], jnp.zeros_like(probs[0, 0]))
    code = gray(lax.axis_index("dp"))
    place = [gray(code ^ bits) * part for bits in range(8)]

    hot = [
        (lax.broadcasted_iota(jnp.int32, (rows, cap), 0) == routed[e][None, :]).astype(BF16)
        for e in each
    ]
    size = 4 * cap
    z_piece, far_a, far_b, mixed_a, mixed_b, near_a, near_b = kernel_call(
        pick_kernel,
        [(2 * size, part)] + [(size, part)] * 2 + [(size + 3 * part * FIRST, part)] * 2 + [(size, part)] * 2,
        routed, tokens, grads, w_in[0], w_out[0],
    )
    split = kernel_call(split_kernel, [(3 * part, part)] * (2 * (CHUNKS - FIRST)), w_in[0], w_out[0])

    def first_weights(mixed, c):
        return mixed[size + 3 * part * c : size + 3 * part * (c + 1)]

    own = {}
    for c in chunks:
        for e, mixed in enumerate((mixed_a, mixed_b)):
            own[c, e] = first_weights(mixed, c) if c < FIRST else split[2 * (c - FIRST) + e]
    got, moved = {(0, 0): near_a, (1, 0): near_b}, {}
    for e, piece in enumerate((mixed_a, mixed_b)):
        mixed = order.send(piece, pairs[e])
        got[1 - e, pairs[e]] = mixed[:size]
        for c in range(FIRST):
            moved[c, e] = first_weights(mixed, c)
    bundle = order.send(z_piece, BIT_Z)
    for e, piece in enumerate((far_a, far_b)):
        got[e, BIT_Z] = bundle[size * e : size * (e + 1)]
        got[e, swaps[e] | BIT_Z] = order.send(piece, swaps[e] | BIT_Z)
    order.take(bundle, *got.values())

    def gathered(e, low):
        return jnp.concatenate(
            [
                jnp.concatenate([got[e, m][low : low + cap], got[e, m][low + 2 * cap : low + 3 * cap]], axis=1)
                for m in members[e]
            ],
            axis=0,
        )

    x_all, y_all = [None] * experts, [None] * experts

    full, near, far_sums, z_sums, mine, theirs = {}, {}, {}, {}, {}, {}
    two, four, every, terms, sent_terms, arrived, theirs_of = {}, {}, {}, {}, {}, {}, {}
    router = [0.0] * experts
    slot_sum = [0.0] * experts

    def send_weights(*which):
        rows_of = 3 * part
        for e in each:
            block = order.send(jnp.concatenate([own[c, e] for c in which], axis=0), pairs[e])
            for i, c in enumerate(which):
                moved[c, e] = block[i * rows_of : (i + 1) * rows_of]

    def take(table, *which):
        order.take(*[table[c, e] for c in which for e in each])

    def partials(c):
        for e in each:
            if c == 0:
                got[e, 0] = order.held(got[e, 0])
                x_all[e], y_all[e] = gathered(e, 0), gathered(e, cap)
            other = order.held(moved[c, e])
            blocks = [
                jnp.concatenate([t[i * part : (i + 1) * part] for t in (own[c, e], other)], axis=0)
                for i in range(3)
            ]
            full[c, e] = blocks
            partial = [dot(x_all[e], blocks[0]), dot(x_all[e], blocks[1]), dot(y_all[e], blocks[2])]
            near[c, e] = [p[: 2 * cap] for p in partial]
            far = jnp.concatenate([p[2 * cap :].astype(BF16) for p in partial], axis=0)
            far_sums[c, e] = order.send(far, swaps[e])

    def second_sums(c):
        take(far_sums, c)
        for e in each:
            near[c, e] = [
                p + far_sums[c, e][2 * cap * i : 2 * cap * (i + 1)].astype(F32)
                for i, p in enumerate(near[c, e])
            ]
        far = jnp.concatenate([p[cap:].astype(BF16) for e in each for p in near[c, e]], axis=0)
        z_sums[c] = order.send(far, BIT_Z)

    def activate(c):
        order.take(z_sums[c])
        parts = []
        for e in each:
            gate, upper, raw = [
                p[:cap] + z_sums[c][(3 * e + i) * cap : (3 * e + i + 1) * cap].astype(F32)
                for i, p in enumerate(near[c, e])
            ]
            sig = jax.nn.sigmoid(gate)
            act = gate * sig * upper
            scale = weight[e][:, None]
            back = raw * scale
            router[e] += jnp.sum(act.astype(BF16).astype(F32) * raw, axis=-1)
            parts += [back * upper * sig * (1.0 + gate * (1.0 - sig)), back * gate * sig, act * scale]
        mine[c] = jnp.concatenate([m.astype(BF16) for m in parts], axis=0)
        theirs[c] = order.send(mine[c], BIT_Z)

    def spread(*which):
        order.take(*[theirs[c] for c in which])
        rows_of = 6 * cap
        for e in each:
            for c in which:
                two[c, e] = jnp.concatenate(
                    [t[3 * cap * e : 3 * cap * (e + 1)].reshape(3, cap, step) for t in (mine[c], theirs[c])],
                    axis=1,
                )
            flat = jnp.concatenate([two[c, e].reshape(-1, step) for c in which], axis=0)
            block = order.send(flat, swaps[e])
            arrived[which, e] = block
            for i, c in enumerate(which):
                four[c, e] = block[i * rows_of : (i + 1) * rows_of]

    down = ((0,), (0,))

    def collect(*which):
        order.take(*[arrived[which, e] for e in each])
        for c in which:
            for e in each:
                every[c, e] = jnp.concatenate([two[c, e], four[c, e].reshape(3, 2 * cap, step)], axis=1)
                for i in range(2):
                    slot_sum[e] += dot(every[c, e][i], full[c, e][i], ((1,), (1,)))

    def weight_grads(*which):
        for e in each:
            far = []
            for c in which:
                dgate, dupper, wact = every[c, e]
                terms[c, e] = [dot(x_all[e], dgate, down), dot(x_all[e], dupper, down), dot(y_all[e], wact, down)]
                far += [t[part:].astype(BF16) for t in terms[c, e]]
            block = order.send(jnp.concatenate(far, axis=0), pairs[e])
            sent_terms[which, e] = block
            for i, c in enumerate(which):
                theirs_of[c, e] = (block, 3 * i)

    def finished(c, e, *before):
        (block, first_part), own_terms = theirs_of[c, e], terms[c, e]
        block = lax.optimization_barrier((block, *before))[0]
        return [
            (t[:part] + block[(first_part + j) * part : (first_part + j + 1) * part].astype(F32)).astype(BF16)
            for j, t in enumerate(own_terms)
        ]

    back = {}

    def send_back():
        low = [slot_sum[e].astype(BF16) for e in each]
        bundle = order.send(jnp.concatenate([low[e][cap : 2 * cap] for e in each], axis=0), BIT_Z)
        order_taken = [bundle]
        for i in (3, 2):
            for e in each:
                m = members[e][i]
                back[e, m] = order.send(low[e][i * cap : (i + 1) * cap], m)
                order_taken.append(back[e, m])
        for e in each:
            back[e, 0] = low[e][:cap]
            back[e, BIT_Z] = bundle[cap * e : cap * (e + 1)]
        order.take(*order_taken)

    def hand_over():
        through = grads.astype(F32)
        for e in each:
            whole = jnp.zeros((cap, width), BF16)
            for m in members[e]:
                whole = lax.dynamic_update_slice(whole, back[e, m][:, :part], (0, place[m]))
                whole = lax.dynamic_update_slice(whole, back[e, m][:, part:], (0, place[m | pairs[e]]))
            through += dot(hot[e], whole)
        return order.send(through.astype(BF16), -1, "pipe")


    partials(0)
    send_weights(2)
    second_sums(0)
    partials(1)
    activate(0)
    take(moved, 2)
    send_weights(3)
    second_sums(1)
    order.take(theirs[0])
    partials(2)
    activate(1)
    take(moved, 3)
    second_sums(2)
    partials(3)
    spread(0, 1)
    activate(2)
    second_sums(3)
    spread(2)
    activate(3)
    collect(0, 1)
    weight_grads(0)
    spread(3)
    collect(2)
    collect(3)
    order.take(sent_terms[(0,), 0], sent_terms[(0,), 1])
    send_back()
    handed = hand_over()
    weight_grads(1, 2)
    weight_grads(3)

    joined = ()
    for which in JOINS:
        done = {(c, e): finished(c, e, *joined) for c in which for e in each}
        joined = join_chunks(which, done, hid, joined)
    router_grad = jnp.where(live, jnp.stack(router), jnp.zeros_like(weight))
    return (
        handed[None],
        joined[0][None],
        joined[1][None],
        router_grad[None, None],
    )


def solution(mesh):
    return jax.shard_map(
        per_device,
        mesh=mesh,
        in_specs=(
            P("pipe", "dp", None),
            P("pipe", "dp", None),
            P("pipe", "dp", None, None),
            P("pipe", "dp", None, None),
            P("pipe", "dp", None, None),
            P("pipe", "dp", None),
            P("pipe", "dp", None, None),
        ),
        out_specs=(
            P("pipe", "dp", None),
            P("pipe", "dp", None, None),
            P("pipe", "dp", None, None),
            P("pipe", "dp", None, None),
        ),
        check_vma=False,
    )
```
